32 devices in a mesh: groups: 2 (over x), seq: 16 (over z, y, core).
Axes of the slice: x: 2, y: 2, z: 4, core: 2. Of those that a mesh axis runs over, the one named last changes fastest.
Arguments:
- tokens: bfloat16 [16384, 3584], P(('groups', 'seq')), parts along dimension 0, may hold values from -600 to 600
- token_request: int32 [16384, 1], P(('groups', 'seq')), parts along dimension 0, may hold values from 0 to 63; in each aligned block of 512 rows (0 to 511, 512 to 1023, ...) at most 32 rows name the same one
- request_slot: int32 [128], P('groups'), parts along dimension 0, may hold values from 0 to 63, each once
- new_rows: bfloat16 [128, 3584], P(('groups', 'seq')), parts along dimension 0, may hold values from -600 to 600
- queries: bfloat16 [128, 3584], P(('groups', 'seq')), parts along dimension 0, may hold values from -120 to 120
- key_cache: bfloat16 [128, 4, 128, 128], P(('groups', 'seq')), parts along dimension 0, may hold values from -6 to 6
- value_cache: bfloat16 [128, 4, 128, 128], P(('groups', 'seq')), parts along dimension 0, may hold values from -6 to 6
- cache_length: int32 [128], P(('groups', 'seq')), parts along dimension 0, may hold values from 2 to 128
- norm_gain: float32 [3584], replicated, may hold values from 0.1 to 1.9
- key_weight: bfloat16 [3584, 512], replicated, may hold values from -0.09375 to 0.09375
- value_weight: bfloat16 [3584, 512], replicated, may hold values from -0.09375 to 0.09375
- key_bias: float32 [512], replicated, may hold values from -3 to 3
- value_bias: float32 [512], replicated, may hold values from -2 to 2
- out_weight: bfloat16 [3584, 3584], P(None, 'seq'), may hold values from -0.09375 to 0.09375
Outputs:
- decoded: bfloat16 [128, 3584], P('groups', 'seq'), parts along dimension 0
The draws below stay inside these ranges and needn't reach their ends.
There are 2 independent parts, one for each index of `groups`. The reference program is written for one: setup_inputs(seed, part) draws one part's arguments, and reference() takes and returns one part's arrays. A program takes and returns all parts, laid end to end along the dimension named above; an argument that names none is the same for every part. Nothing has to cross between parts.
Inputs may be any that keep to these rules, and one draw needn't show every extreme that they name: `token_request`: of the 512 tokens of one device, at most 32 belong to one request. `request_slot`: A permutation of the 64 slots.
All inputs are finite; a program needn't handle non-finite values.
Results may differ from the reference program's by a relative error of at most 0.013.
Values may be sent and summed in bfloat16 or wider, within the bound.
A program may use at most 64 MiB of HBM per device.

```python
import math
import jax
import jax.numpy as jnp
import numpy as np
from jax import lax

D = 3584
HEADS = 28
KV_HEADS = 4
HEAD_DIM = 128
TOK_DEV = 512
CACHE = 128
GROUP = 7
KV_WIDTH = 512
TOKENS = 8192
REQS = 64
CAP = 32


def draw_queries(key, part):
    key = jax.random.fold_in(key, 12)
    field = jnp.clip(jax.random.normal(key, (REQS, HEADS * HEAD_DIM), jnp.float32), -6.0, 6.0) * 2.5
    return field.astype(jnp.bfloat16)


def draw_key_cache(key, part):
    key = jax.random.fold_in(key, 11)
    cache_keys = jnp.clip(jax.random.normal(key, (REQS, KV_HEADS, CACHE, HEAD_DIM), jnp.float32), -6.0, 6.0)
    return cache_keys.astype(jnp.bfloat16)


def draw_tokens(key, part):
    key = jax.random.fold_in(key, 13)
    row_scale = jnp.exp(jax.random.uniform(jax.random.fold_in(key, 1), (TOKENS, 1), jnp.float32, 0.0, math.log(10.0)))
    col_scale = jnp.exp(jax.random.uniform(jax.random.fold_in(key, 2), (1, D), jnp.float32, 0.0, math.log(10.0)))
    base_field = jnp.clip(jax.random.normal(jax.random.fold_in(key, 3), (TOKENS, D), jnp.float32), -6.0, 6.0)
    return (base_field * row_scale * col_scale).astype(jnp.bfloat16)


def draw_new_rows(key, part):
    key = jax.random.fold_in(key, 14)
    row_scale = jnp.exp(jax.random.uniform(jax.random.fold_in(key, 1), (REQS, 1), jnp.float32, 0.0, math.log(10.0)))
    col_scale = jnp.exp(jax.random.uniform(jax.random.fold_in(key, 2), (1, D), jnp.float32, 0.0, math.log(10.0)))
    base_field = jnp.clip(jax.random.normal(jax.random.fold_in(key, 3), (REQS, D), jnp.float32), -6.0, 6.0)
    return (base_field * row_scale * col_scale).astype(jnp.bfloat16)


def draw_cache_length(key, part):
    key = jax.random.fold_in(key, 15)
    lengths = jax.random.randint(jax.random.fold_in(key, 1), (REQS,), 2, CACHE + 1)
    longest = jax.random.randint(jax.random.fold_in(key, 2), (), 0, REQS)
    return lengths.at[longest].set(CACHE).astype(jnp.int32)


def steps_of(key, dims, pieces, smallest, top_value):
    gain, own = 1.0, jax.random.fold_in(key, 6)
    for axis_at, shards_of in pieces:
        steps = jnp.exp(jax.random.uniform(jax.random.fold_in(own, axis_at), (shards_of,), jnp.float32, smallest / len(pieces), top_value / len(pieces)))
        gain = gain * jnp.repeat(steps, dims[axis_at] // shards_of).reshape([-1 if axis == axis_at else 1 for axis in range(len(dims))])
    return gain


def assign_block(stream_key, own, number, rows, count, top, most, lean):
    ranking = jax.random.permutation(stream_key, count)
    heavy_load, ordinary = shares(count, rows * top, most, lean, True), shares(count, rows * top, most, lean, False)
    places = jnp.arange(count)

    def named(tallies, rotation):
        used = int((tallies > 0).sum())
        fixed = max(1, used // 4)
        passed = fixed + (places - fixed + rotation * (used - fixed)) % max(1, count - fixed)
        return jnp.zeros((count,), jnp.int32).at[ranking[jnp.where(places < fixed, places, passed)]].set(jnp.asarray(tallies, jnp.int32))

    tallies = jnp.where(number % 4 == 0, named(heavy_load, number // 4), named(ordinary, number - number // 4 - 1))
    mixed = jax.random.permutation(jax.random.fold_in(own, 3), count)
    source_of, taker = mixed[0:count // 2 * 2:2], mixed[1:count // 2 * 2:2]
    room = jnp.minimum(tallies[source_of] - 1, most - tallies[taker]) // 2
    room = jnp.where((source_of == ranking[0]) | (taker == ranking[0]) | (tallies[taker] == 0), 0, jnp.maximum(room, 0))
    passed = jax.random.randint(jax.random.fold_in(own, 4), (count // 2,), 0, 1 << 20) % (room + 1)
    tallies = tallies.at[source_of].add(-passed).at[taker].add(passed)
    labels = jnp.searchsorted(jnp.cumsum(tallies), jnp.arange(rows * top), side="right").astype(jnp.int32)
    table = labels.reshape(top, rows).T
    table = table[jax.random.permutation(jax.random.fold_in(own, 1), rows)]
    rotation = jax.random.randint(jax.random.fold_in(own, 2), (rows, 1), 0, top)
    return jnp.take_along_axis(table, (jnp.arange(top)[None, :] + rotation) % top, axis=1)


def shares(number_of, total, bound, lean, full):
    portions = [(1 << 20) // math.isqrt(rank ** lean) + 1 for rank in range(1, number_of + 1)]
    largest = bound if full else min(bound, max(-(-total // number_of), total * portions[0] // sum(portions)))
    least = 1 if total - largest >= number_of - 1 else 0
    given, rest = [largest] + [least] * (number_of - 1), total - largest - least * (number_of - 1)
    while rest > 0:
        candidates = [i for i in range(1, number_of) if given[i] < largest] or [i for i in range(1, number_of) if given[i] < bound]
        mass, budget = sum([portions[i] for i in candidates]), rest
        for i in candidates:
            more = min(bound - given[i], max(1, budget * portions[i] // mass), rest)
            given[i] = given[i] + more
            rest = rest - more
    return np.array(given)


def noise(rng, shape, deviation, bound, split=(), held_as=jnp.bfloat16):
    result = jax.random.normal(rng, shape, jnp.float32) * deviation
    if len(split) > 0:
        result = steps_of(rng, shape, split, -0.22, 0.18) * result
    return jnp.clip(result, min=-bound, max=bound).astype(held_as)


def setup_inputs(seed: int = 0, part: int = 0) -> dict:
    keys = jax.random.split(jax.random.key(seed), 15)
    part_splits = jax.random.split(jax.random.fold_in(keys[14], part), 15)
    tokens = draw_tokens(jax.random.fold_in(jax.random.fold_in(keys[14], part), 71), part)
    token_request_keys = jax.random.split(jax.random.fold_in(part_splits[1], 1), TOKENS // TOK_DEV)
    token_request_turns = jax.random.permutation(jax.random.fold_in(part_splits[1], 3), TOKENS // TOK_DEV)
    token_request = jax.vmap(lambda own, number: assign_block(jax.random.fold_in(part_splits[1], 2), own, number, TOK_DEV, REQS, 1, CAP, 2))(token_request_keys, token_request_turns).reshape((TOKENS, 1))
    request_slot = jax.random.permutation(part_splits[2], REQS).astype(jnp.int32)
    new_rows = draw_new_rows(jax.random.fold_in(jax.random.fold_in(keys[14], part), 71), part)
    queries = draw_queries(jax.random.fold_in(jax.random.fold_in(keys[14], part), 71), part)
    key_cache = draw_key_cache(jax.random.fold_in(jax.random.fold_in(keys[14], part), 71), part)
    value_cache = noise(part_splits[6], (REQS, KV_HEADS, CACHE, HEAD_DIM), 1.0, 6.0, ((0, 16),))
    cache_length = draw_cache_length(jax.random.fold_in(jax.random.fold_in(keys[14], part), 71), part)
    norm_gain = jnp.clip(1.0 + 0.18 * jax.random.normal(keys[8], (D,), jnp.float32), 0.1, 1.9)
    key_weight = noise(keys[9], (D, KV_WIDTH), D ** -0.5, 0.09375)
    value_weight = noise(keys[10], (D, KV_WIDTH), D ** -0.5, 0.09375)
    key_bias = noise(keys[11], (KV_WIDTH,), 0.5, 3.0, (), jnp.float32)
    value_bias = noise(keys[12], (KV_WIDTH,), 0.3, 2.0, (), jnp.float32)
    out_weight = noise(keys[13], (HEADS * HEAD_DIM, D), (HEADS * HEAD_DIM) ** -0.5, 0.09375, ((1, 16),))
    return {"tokens": tokens, "token_request": token_request, "request_slot": request_slot, "new_rows": new_rows, "queries": queries, "key_cache": key_cache, "value_cache": value_cache, "cache_length": cache_length, "norm_gain": norm_gain, "key_weight": key_weight, "value_weight": value_weight, "key_bias": key_bias, "value_bias": value_bias, "out_weight": out_weight}


def project(row_data, norm_gain, key_weight, value_weight, key_bias, value_bias):
    widened = row_data.astype(jnp.float32)
    power = lax.optimization_barrier(jnp.mean(widened * widened, axis=-1, keepdims=True))
    normed = (widened * lax.rsqrt(power + 1e-06) * norm_gain).astype(jnp.bfloat16)
    new_keys = (jnp.dot(normed, key_weight, preferred_element_type=jnp.float32) + key_bias).astype(jnp.bfloat16)
    new_values = (jnp.dot(normed, value_weight, preferred_element_type=jnp.float32) + value_bias).astype(jnp.bfloat16)
    return (new_keys, new_values)

def rounded_back(weights):
    return lax.optimization_barrier(weights.astype(jnp.bfloat16)).astype(jnp.float32)

def reference(tokens, token_request, request_slot, new_rows, queries, key_cache, value_cache, cache_length, norm_gain, key_weight, value_weight, key_bias, value_bias, out_weight):
    score_scale = HEAD_DIM ** (-0.5)
    fresh_keys, fresh_values = project(tokens, norm_gain, key_weight, value_weight, key_bias, value_bias)
    own_keys, own_values = project(new_rows, norm_gain, key_weight, value_weight, key_bias, value_bias)
    token_slot = request_slot[token_request[:, 0]].astype(jnp.int32)
    grouped = queries.astype(jnp.float32).reshape(REQS, KV_HEADS, GROUP, HEAD_DIM)
    cache_scores = jnp.einsum('rgjd,rgcd->rgjc', grouped, key_cache.astype(jnp.float32)) * score_scale
    visible = jnp.arange(CACHE, dtype=jnp.int32)[None, None, None, :] < cache_length[:, None, None, None]
    cache_scores = jnp.where(visible, cache_scores, -jnp.inf)
    own_scores = jnp.einsum('rgjd,rgd->rgj', grouped, own_keys.astype(jnp.float32).reshape(REQS, KV_HEADS, HEAD_DIM)) * score_scale
    token_queries = grouped[token_slot]
    token_scores = jnp.einsum('tgjd,tgd->tgj', token_queries, fresh_keys.astype(jnp.float32).reshape(TOKENS, KV_HEADS, HEAD_DIM)) * score_scale
    slot_top = jax.ops.segment_max(token_scores, token_slot, num_segments=REQS)
    row_top = jnp.maximum(jnp.maximum(lax.optimization_barrier(jnp.max(cache_scores, axis=-1)), own_scores), slot_top)
    cache_weights = jnp.exp(cache_scores - row_top[..., None])
    own_weights = jnp.exp(own_scores - row_top)
    token_weights = jnp.exp(token_scores - row_top[token_slot])
    totals = lax.optimization_barrier(jnp.sum(cache_weights, axis=-1)) + own_weights + jax.ops.segment_sum(token_weights, token_slot, num_segments=REQS)
    weighted_sum = jnp.einsum('rgjc,rgcd->rgjd', rounded_back(cache_weights), value_cache.astype(jnp.float32))
    weighted_sum = weighted_sum + rounded_back(own_weights)[..., None] * own_values.astype(jnp.float32).reshape(REQS, KV_HEADS, 1, HEAD_DIM)
    token_terms = rounded_back(token_weights)[..., None] * fresh_values.astype(jnp.float32).reshape(TOKENS, KV_HEADS, 1, HEAD_DIM)
    weighted_sum = weighted_sum + jax.ops.segment_sum(token_terms, token_slot, num_segments=REQS)
    head_outputs = (weighted_sum / totals[..., None]).astype(jnp.bfloat16).reshape(REQS, HEADS * HEAD_DIM)
    return jnp.dot(head_outputs, out_weight, preferred_element_type=jnp.float32).astype(jnp.bfloat16)
```

```python
import functools

import jax
import jax.numpy as jnp
from jax import lax
from jax.experimental import pallas as pl
from jax.experimental.pallas import tpu as pltpu
from jax.sharding import PartitionSpec as P

MESH = pl.DeviceIdType.MESH
NT = (((1,), (1,)), ((), ()))
LOW = -1e30


def kernel(
    dims,
    token_request,
    request_slot,
    new_rows,
    queries,
    cache_length,
    norm_gain,
    key_bias,
    value_bias,
    tokens_hbm,
    key_weight_hbm,
    value_weight_hbm,
    out_weight_hbm,
    key_cache_hbm,
    value_cache_hbm,
    out,
    tok,
    kw,
    vw,
    ow,
    kc,
    vc,
    xn,
    qstage,
    qall,
    slots,
    kvl,
    kvr,
    part,
    rpart,
    stat,
    rstat,
    hstage,
    hall,
    load_sem,
    qs_sem,
    qr_sem,
    sib_s,
    sib_r,
    ps_sem,
    pr_sem,
    ss_sem,
    sr_sem,
    hs_sem,
    hr_sem,
    fs_sem,
    fr_sem,
):
    nk, rows_here, kv_heads, group, head_dim = dims
    f32, bf16 = jnp.float32, jnp.bfloat16
    tok_dev, width = tok.shape
    block = qall.shape[2]
    chunks = 4
    chunk = tok_dev // chunks
    me = lax.axis_index("seq")
    mek, mec = me // 2, me % 2
    sibling = mek * 2 + (1 - mec)

    def ahead(i):
        return lax.rem(mek + i, nk)

    def behind(i):
        return lax.rem(mek + nk - i, nk)

    def peer(k):
        return {"seq": k * 2 + mec}

    loads = []

    def load(src, dst):
        c = pltpu.make_async_copy(src, dst, load_sem.at[len(loads)])
        c.start()
        loads.append(c)
        return c

    tok_loads = [
        load(tokens_hbm.at[pl.ds(c * chunk, chunk)], tok.at[pl.ds(c * chunk, chunk)])
        for c in range(chunks)
    ]
    kw_load = load(key_weight_hbm, kw)
    vw_load = load(value_weight_hbm, vw)
    kc_load = load(key_cache_hbm, kc)
    vc_load = load(value_cache_hbm, vc)
    ow_load = load(out_weight_hbm, ow)

    barrier = pltpu.get_barrier_semaphore()
    pl.semaphore_signal(barrier, inc=1, device_id={"seq": sibling}, device_id_type=MESH)
    for i in range(1, nk):
        pl.semaphore_signal(barrier, inc=1, device_id=peer(ahead(i)), device_id_type=MESH)

    qstage[...] = jnp.zeros_like(qstage)
    q_wide = queries[...].astype(f32)
    for g in range(kv_heads):
        for j in range(group):
            h = g * group + j
            qstage[g, j * rows_here : (j + 1) * rows_here, :] = q_wide[
                :, h * head_dim : (h + 1) * head_dim
            ]
    for g in range(kv_heads):
        qall[0, g] = qstage[g].astype(bf16)

    slot_total = request_slot.shape[0]
    matches = token_request[...] == lax.broadcasted_iota(jnp.int32, (slot_total, tok_dev), 0)
    slot_row = jnp.sum(
        jnp.where(matches, request_slot[...].astype(f32), 0.0), axis=0, keepdims=True
    ).astype(jnp.int32)
    slots[0] = jnp.broadcast_to(slot_row, (8, tok_dev))

    pl.semaphore_wait(barrier, nk)

    def remote(src, dst, s, r, device):
        c = pltpu.make_async_remote_copy(
            src_ref=src, dst_ref=dst, send_sem=s, recv_sem=r, device_id=device, device_id_type=MESH
        )
        c.start()
        return c

    started = []
    q_copies = {}
    for i in range(1, nk):
        q_copies[i] = remote(qall.at[0], qall.at[i], qs_sem.at[i], qr_sem.at[i], peer(ahead(i)))
    slot_copy = remote(slots.at[0], slots.at[1], sib_s.at[2], sib_r.at[2], {"seq": sibling})

    gain = norm_gain[...]

    def normed(x):
        power = jnp.mean(x * x, axis=-1, keepdims=True)
        return (x * lax.rsqrt(power + 1e-06) * gain).astype(bf16)

    fresh = jnp.concatenate(
        [new_rows[...].astype(f32), jnp.zeros((16 - rows_here, width), f32)], axis=0
    )
    xn[tok_dev : tok_dev + 16, :] = normed(fresh)
    for c in range(chunks):
        tok_loads[c].wait()

        @pl.loop(c * chunk // 16, (c + 1) * chunk // 16)
        def _(b):
            at = pl.ds(pl.multiple_of(b * 16, 16), 16)
            xn[at, :] = normed(tok[at, :].astype(f32))

    kv_copies = []
    half = kw.shape[1] // 2
    for hf in range(2):
        cols = slice(hf * half, (hf + 1) * half)
        for n, (w, b, w_load) in enumerate(((kw, key_bias, kw_load), (vw, value_bias, vw_load))):
            if hf == 0:
                w_load.wait()
            kvl[hf, :, n * half : (n + 1) * half] = (
                jnp.dot(xn[...], w[:, cols], preferred_element_type=f32) + b[:, cols]
            ).astype(bf16)
        kv_copies.append(
            remote(
                kvl.at[hf, pl.ds(0, tok_dev)],
                kvr.at[hf],
                sib_s.at[hf],
                sib_r.at[hf],
                {"seq": sibling},
            )
        )

    for i in range(1, nk):
        q_copies[i].wait_recv()
    slot_copy.wait_recv()

    scale = head_dim ** (-0.5)
    per_half = kv_heads // 2
    per_chunk = min(4, nk)
    chunk_rows = per_chunk * block
    p_copies = {}
    for hf in range(2):
        kv_copies[hf].wait_recv()
        for q0 in range(0, nk, per_chunk):
            lane = lax.broadcasted_iota(jnp.int32, (block, 128), 0) % rows_here
            row_slot = jnp.concatenate(
                [(behind(q0 + i) * 2 + mec) * rows_here + lane for i in range(per_chunk)], axis=0
            )[:, :1]
            mask_l = row_slot == slots[0, 0:1, :]
            mask_r = row_slot == slots[1, 0:1, :]
            lses = []
            for gl in range(per_half):
                g = hf * per_half + gl
                q = qall[q0 : q0 + per_chunk, g].reshape(chunk_rows, head_dim)
                kcols = slice(gl * head_dim, (gl + 1) * head_dim)
                vcols = slice(half + gl * head_dim, half + (gl + 1) * head_dim)
                s_l = lax.dot_general(q, kvl[hf, :tok_dev, kcols], NT, preferred_element_type=f32)
                s_r = lax.dot_general(q, kvr[hf, :, kcols], NT, preferred_element_type=f32)
                s_l = jnp.where(mask_l, s_l * scale, LOW)
                s_r = jnp.where(mask_r, s_r * scale, LOW)
                top = jnp.max(jnp.maximum(s_l, s_r), axis=-1, keepdims=True)
                p_l = jnp.exp(s_l - top)
                p_r = jnp.exp(s_r - top)
                total = jnp.sum(p_l + p_r, axis=-1, keepdims=True)
                o = jnp.dot(
                    p_l.astype(bf16), kvl[hf, :tok_dev, vcols], preferred_element_type=f32
                ) + jnp.dot(p_r.astype(bf16), kvr[hf, :, vcols], preferred_element_type=f32)
                o = (o / total).astype(bf16)
                part[hf, q0 : q0 + per_chunk, gl] = o.reshape(per_chunk, block, head_dim)
                lses.append(top + jnp.log(total))
            which = lax.broadcasted_iota(jnp.int32, (chunk_rows, 128), 1)
            packed = jnp.where(which == 0, lses[0], jnp.where(which == 1, lses[1], 0.0))
            stat[hf, q0 // per_chunk] = packed.T[:8, :]
            for i in range(q0, q0 + per_chunk):
                if i > 0:
                    p_copies[hf, i] = (
                        remote(
                            part.at[hf, i],
                            rpart.at[hf, i],
                            ps_sem.at[hf, i],
                            pr_sem.at[hf, i],
                            peer(behind(i)),
                        ),
                        remote(
                            stat.at[hf, i // per_chunk],
                            rstat.at[hf, i],
                            ss_sem.at[hf, i],
                            sr_sem.at[hf, i],
                            peer(behind(i)),
                        ),
                    )

    kc_load.wait()
    vc_load.wait()
    row_of = lax.broadcasted_iota(jnp.int32, (block, 128), 0) % rows_here
    place = lax.broadcasted_iota(jnp.int32, (block, 128), 1)
    visible = [(row_of == r) & (place < cache_length[r]) for r in range(rows_here)]
    own = []
    for g in range(kv_heads):
        hf, gl = g // per_half, g % per_half
        q = qall[0, g]
        s_c = jnp.full((block, 128), LOW, f32)
        for r in range(rows_here):
            s = lax.dot_general(q, kc[r, g], NT, preferred_element_type=f32) * scale
            s_c = jnp.where(visible[r], s, s_c)
        new = kvl[hf, tok_dev : tok_dev + 16, :].astype(f32)[:rows_here]
        k_new = new[:, gl * head_dim : (gl + 1) * head_dim]
        v_new = new[:, half + gl * head_dim : half + (gl + 1) * head_dim]
        k_new = jnp.concatenate([k_new] * (block // rows_here), axis=0)
        v_new = jnp.concatenate([v_new] * (block // rows_here), axis=0)
        s_o = jnp.sum(q.astype(f32) * k_new, axis=-1, keepdims=True) * scale
        top = jnp.maximum(jnp.max(s_c, axis=-1, keepdims=True), s_o)
        p_c = jnp.exp(s_c - top)
        p_o = jnp.exp(s_o - top)
        total = jnp.sum(p_c, axis=-1, keepdims=True) + p_o
        acc = p_o.astype(bf16).astype(f32) * v_new
        for r in range(rows_here):
            acc = acc + jnp.dot(
                jnp.where(row_of == r, p_c, 0.0).astype(bf16), vc[r, g], preferred_element_type=f32
            )
        own.append((top, total, acc))

    for hf in range(2):
        for i in range(1, nk):
            for c in p_copies[hf, i]:
                c.wait_recv()
        rstat[hf, 0] = stat[hf, 0]
        flat = rstat[hf].reshape(nk * 8, 128)
        pad = -(nk * 8) % 128
        if pad:
            flat = jnp.concatenate([flat, jnp.zeros((pad, 128), f32)], axis=0)
        turned = flat.T
        for gl in range(per_half):
            g = hf * per_half + gl
            top, total, acc = own[g]
            cols = []
            for i in range(nk):
                r0 = (i % per_chunk) * block
                cols.append(turned[r0 : r0 + block, i * 8 + gl : i * 8 + gl + 1])
            best = top
            for col in cols:
                best = jnp.maximum(best, col)
            w = jnp.exp(top - best)
            total = total * w
            acc = acc * w
            for i in range(nk):
                w = jnp.exp(cols[i] - best)
                total = total + w
                piece = part[hf, 0, gl] if i == 0 else rpart[hf, i, gl]
                acc = acc + w * piece.astype(f32)
            result = acc / total
            for j in range(group):
                hstage[
                    g * rows_here : (g + 1) * rows_here, j * head_dim : (j + 1) * head_dim
                ] = result[j * rows_here : (j + 1) * rows_here, :]
    hall[me] = hstage[...].astype(bf16)

    h_copies = {}
    for i in range(1, nk):
        h_copies[i] = remote(
            hall.at[me], hall.at[me], hs_sem.at[i], hr_sem.at[i], peer(ahead(i))
        )
    f_copies = {}
    f_copies[0] = remote(hall.at[me], hall.at[me], fs_sem.at[0], fr_sem.at[0], {"seq": sibling})
    for i in range(1, nk):
        h_copies[i].wait_recv()
        at = behind(i) * 2 + mec
        f_copies[i] = remote(
            hall.at[at], hall.at[at], fs_sem.at[i], fr_sem.at[i], {"seq": sibling}
        )
    ow_load.wait()
    for i in range(nk):
        f_copies[i].wait_recv()

    rows_all = hall.shape[0] * 16
    flat = hall[...].reshape(rows_all, hall.shape[2])
    slot_at = lax.broadcasted_iota(jnp.int32, (slot_total, rows_all), 0)
    row_at = lax.broadcasted_iota(jnp.int32, (slot_total, rows_all), 1)
    acc = None
    for g in range(kv_heads):
        want = (slot_at // rows_here) * 16 + g * rows_here + slot_at % rows_here
        pick = jnp.where(row_at == want, 1.0, 0.0).astype(bf16)
        a = jnp.dot(pick, flat, preferred_element_type=f32).astype(bf16)
        span = group * head_dim
        term = jnp.dot(a, ow[g * span : (g + 1) * span, :], preferred_element_type=f32)
        acc = term if acc is None else acc + term
    out[...] = acc.astype(bf16)

    for i in range(1, nk):
        q_copies[i].wait_send()
        h_copies[i].wait_send()
        for hf in range(2):
            for c in p_copies[hf, i]:
                c.wait_send()
    for i in range(nk):
        f_copies[i].wait_send()
    slot_copy.wait_send()
    for c in kv_copies:
        c.wait_send()


def body(
    tokens,
    token_request,
    request_slot,
    new_rows,
    queries,
    key_cache,
    value_cache,
    cache_length,
    norm_gain,
    key_weight,
    value_weight,
    key_bias,
    value_bias,
    out_weight,
):
    seq_count = lax.axis_size("seq")
    nk = seq_count // 2
    rows_here, kv_heads, cache_size, head_dim = key_cache.shape
    slot_count = request_slot.shape[0]
    tok_dev, width = tokens.shape
    group = queries.shape[1] // (kv_heads * head_dim)
    kv_width = kv_heads * head_dim
    block = 32
    f32, bf16, i32 = jnp.float32, jnp.bfloat16, jnp.int32
    vmem = pl.BlockSpec(memory_space=pltpu.VMEM)
    smem = pl.BlockSpec(memory_space=pltpu.SMEM)
    hbm = pl.BlockSpec(memory_space=pl.ANY)
    dma = pltpu.SemaphoreType.DMA
    dims = (nk, rows_here, kv_heads, group, head_dim)
    return pl.pallas_call(
        functools.partial(kernel, dims),
        out_shape=jax.ShapeDtypeStruct((slot_count, out_weight.shape[1]), bf16),
        in_specs=[vmem, vmem, vmem, vmem, smem, vmem, vmem, vmem] + [hbm] * 6,
        out_specs=vmem,
        scratch_shapes=[
            pltpu.VMEM((tok_dev, width), bf16),
            pltpu.VMEM((width, kv_width), bf16),
            pltpu.VMEM((width, kv_width), bf16),
            pltpu.VMEM(out_weight.shape, bf16),
            pltpu.VMEM(key_cache.shape, bf16),
            pltpu.VMEM(value_cache.shape, bf16),
            pltpu.VMEM((tok_dev + 16, width), bf16),
            pltpu.VMEM((kv_heads, block, head_dim), f32),
            pltpu.VMEM((nk, kv_heads, block, head_dim), bf16),
            pltpu.VMEM((2, 8, tok_dev), i32),
            pltpu.VMEM((2, tok_dev + 16, kv_width), bf16),
            pltpu.VMEM((2, tok_dev, kv_width), bf16),
            pltpu.VMEM((2, nk, kv_heads // 2, block, head_dim), bf16),
            pltpu.VMEM((2, nk, kv_heads // 2, block, head_dim), bf16),
            pltpu.VMEM((2, nk // 4, 8, 128), f32),
            pltpu.VMEM((2, nk, 8, 128), f32),
            pltpu.VMEM((16, group * head_dim), f32),
            pltpu.VMEM((seq_count, 16, group * head_dim), bf16),
            dma((9,)),
            dma((nk,)),
            dma((nk,)),
            dma((3,)),
            dma((3,)),
            dma((2, nk)),
            dma((2, nk)),
            dma((2, nk)),
            dma((2, nk)),
            dma((nk,)),
            dma((nk,)),
            dma((nk,)),
            dma((nk,)),
        ],
        compiler_params=pltpu.CompilerParams(
            collective_id=0, has_side_effects=True, vmem_limit_bytes=52 * 1024 * 1024
        ),
    )(
        token_request.reshape(1, tok_dev),
        request_slot.reshape(slot_count, 1),
        new_rows,
        queries,
        cache_length,
        norm_gain.reshape(1, width),
        key_bias.reshape(1, kv_width),
        value_bias.reshape(1, kv_width),
        tokens,
        key_weight,
        value_weight,
        out_weight,
        key_cache,
        value_cache,
    )


def solution(mesh):
    in_specs = (
        P(("groups", "seq"), None),
        P(("groups", "seq"), None),
        P("groups"),
        P(("groups", "seq"), None),
        P(("groups", "seq"), None),
        P(("groups", "seq"), None, None, None),
        P(("groups", "seq"), None, None, None),
        P(("groups", "seq")),
        P(),
        P(),
        P(),
        P(),
        P(),
        P(None, "seq"),
    )
    out_specs = P("groups", "seq")
    return jax.shard_map(body, mesh=mesh, in_specs=in_specs, out_specs=out_specs, check_vma=False)
```

```python
import functools

import jax
import jax.numpy as jnp
from jax import lax
from jax.experimental import pallas as pl
from jax.experimental.pallas import tpu as pltpu
from jax.sharding import PartitionSpec as P

MESH = pl.DeviceIdType.MESH
NT = (((1,), (1,)), ((), ()))
LOW = -1e30


def kernel(
    dims,
    token_request_hbm,
    request_slot_hbm,
    new_rows_hbm,
    queries_hbm,
    cache_length_hbm,
    norm_gain_hbm,
    key_bias_hbm,
    value_bias_hbm,
    tokens_hbm,
    key_weight_hbm,
    value_weight_hbm,
    out_weight_hbm,
    key_cache_hbm,
    value_cache_hbm,
    out,
    token_request,
    request_slot,
    new_rows,
    queries,
    cache_length,
    norm_gain,
    key_bias,
    value_bias,
    gain_row,
    tok,
    kw,
    vw,
    ow,
    kc,
    vc,
    xn,
    qstage,
    qall,
    slots,
    kvl,
    kvr,
    part,
    rpart,
    stat,
    rstat,
    hstage,
    hall,
    load_sem,
    qs_sem,
    qr_sem,
    sib_s,
    sib_r,
    ps_sem,
    pr_sem,
    ss_sem,
    sr_sem,
    hs_sem,
    hr_sem,
    fs_sem,
    fr_sem,
):
    nk, rows_here, kv_heads, group, head_dim = dims
    f32, bf16 = jnp.float32, jnp.bfloat16
    tok_dev, width = tok.shape
    block = qall.shape[2]
    chunks = 4
    chunk = tok_dev // chunks
    me = lax.axis_index("seq")
    mek, mec = me // 2, me % 2
    sibling = mek * 2 + (1 - mec)

    def ahead(i):
        return lax.rem(mek + i, nk)

    def behind(i):
        return lax.rem(mek + nk - i, nk)

    def peer(k):
        return {"seq": k * 2 + mec}

    loads = []

    def load(src, dst):
        c = pltpu.make_async_copy(src, dst, load_sem.at[len(loads)])
        c.start()
        loads.append(c)
        return c

    q_load = load(queries_hbm, queries)
    request_load = load(token_request_hbm, token_request)
    slot_load = load(request_slot_hbm, request_slot)
    small_loads = [
        load(norm_gain_hbm, norm_gain),
        load(new_rows_hbm, new_rows),
        load(cache_length_hbm, cache_length),
        load(key_bias_hbm, key_bias),
        load(value_bias_hbm, value_bias),
    ]
    tok_loads = [
        load(tokens_hbm.at[pl.ds(c * chunk, chunk)], tok.at[pl.ds(c * chunk, chunk)])
        for c in range(chunks)
    ]
    kw_load = load(key_weight_hbm, kw)
    vw_load = load(value_weight_hbm, vw)
    kc_load = load(key_cache_hbm, kc)
    vc_load = load(value_cache_hbm, vc)
    ow_load = load(out_weight_hbm, ow)

    barrier = pltpu.get_barrier_semaphore()
    pl.semaphore_signal(barrier, inc=1, device_id={"seq": sibling}, device_id_type=MESH)
    for i in range(1, nk):
        pl.semaphore_signal(barrier, inc=1, device_id=peer(ahead(i)), device_id_type=MESH)

    qstage[...] = jnp.zeros_like(qstage)
    q_load.wait()
    q_wide = queries[...].astype(f32)
    for g in range(kv_heads):
        for j in range(group):
            h = g * group + j
            qstage[g, j * rows_here : (j + 1) * rows_here, :] = q_wide[
                :, h * head_dim : (h + 1) * head_dim
            ]
    for g in range(kv_heads):
        qall[0, g] = qstage[g].astype(bf16)

    slot_total = request_slot.shape[1]
    request_load.wait()
    slot_load.wait()
    square = (slot_total, slot_total)
    slot_column = jnp.sum(
        jnp.where(
            lax.broadcasted_iota(jnp.int32, square, 0) == lax.broadcasted_iota(jnp.int32, square, 1),
            request_slot[...].astype(f32),
            0.0,
        ),
        axis=1,
        keepdims=True,
    )
    matches = token_request[...] == lax.broadcasted_iota(jnp.int32, (slot_total, tok_dev), 0)
    slot_row = jnp.sum(
        jnp.where(matches, slot_column, 0.0), axis=0, keepdims=True
    ).astype(jnp.int32)
    slots[0] = jnp.broadcast_to(slot_row, (8, tok_dev))

    pl.semaphore_wait(barrier, nk)

    def remote(src, dst, s, r, device):
        c = pltpu.make_async_remote_copy(
            src_ref=src, dst_ref=dst, send_sem=s, recv_sem=r, device_id=device, device_id_type=MESH
        )
        c.start()
        return c

    started = []
    q_copies = {}
    for i in range(1, nk):
        q_copies[i] = remote(qall.at[0], qall.at[i], qs_sem.at[i], qr_sem.at[i], peer(ahead(i)))
    slot_copy = remote(slots.at[0], slots.at[1], sib_s.at[2], sib_r.at[2], {"seq": sibling})

    for c in small_loads:
        c.wait()
    lanes = norm_gain.shape[1]
    for n in range(norm_gain.shape[0]):
        gain_row[:, n * lanes : (n + 1) * lanes] = norm_gain[n : n + 1, :]
    gain = gain_row[...]

    def normed(x):
        power = jnp.mean(x * x, axis=-1, keepdims=True)
        return (x * lax.rsqrt(power + 1e-06) * gain).astype(bf16)

    fresh = jnp.concatenate(
        [new_rows[...].astype(f32), jnp.zeros((16 - rows_here, width), f32)], axis=0
    )
    xn[tok_dev : tok_dev + 16, :] = normed(fresh)
    for c in range(chunks):
        tok_loads[c].wait()

        @pl.loop(c * chunk // 16, (c + 1) * chunk // 16)
        def _(b):
            at = pl.ds(pl.multiple_of(b * 16, 16), 16)
            xn[at, :] = normed(tok[at, :].astype(f32))

    kv_copies = []
    half = kw.shape[1] // 2
    for hf in range(2):
        cols = slice(hf * half, (hf + 1) * half)
        for n, (w, b, w_load) in enumerate(((kw, key_bias, kw_load), (vw, value_bias, vw_load))):
            if hf == 0:
                w_load.wait()
            kvl[hf, :, n * half : (n + 1) * half] = (
                jnp.dot(xn[...], w[:, cols], preferred_element_type=f32) + b[:, cols]
            ).astype(bf16)
        kv_copies.append(
            remote(
                kvl.at[hf, pl.ds(0, tok_dev)],
                kvr.at[hf],
                sib_s.at[hf],
                sib_r.at[hf],
                {"seq": sibling},
            )
        )

    for i in range(1, nk):
        q_copies[i].wait_recv()
    slot_copy.wait_recv()

    scale = head_dim ** (-0.5)
    per_half = kv_heads // 2
    per_chunk = min(4, nk)
    chunk_rows = per_chunk * block
    p_copies = {}
    for hf in range(2):
        kv_copies[hf].wait_recv()
        for q0 in range(0, nk, per_chunk):
            lane = lax.broadcasted_iota(jnp.int32, (block, 128), 0) % rows_here
            row_slot = jnp.concatenate(
                [(behind(q0 + i) * 2 + mec) * rows_here + lane for i in range(per_chunk)], axis=0
            )[:, :1]
            mask_l = row_slot == slots[0, 0:1, :]
            mask_r = row_slot == slots[1, 0:1, :]
            lses = []
            for gl in range(per_half):
                g = hf * per_half + gl
                q = qall[q0 : q0 + per_chunk, g].reshape(chunk_rows, head_dim)
                kcols = slice(gl * head_dim, (gl + 1) * head_dim)
                vcols = slice(half + gl * head_dim, half + (gl + 1) * head_dim)
                s_l = lax.dot_general(q, kvl[hf, :tok_dev, kcols], NT, preferred_element_type=f32)
                s_r = lax.dot_general(q, kvr[hf, :, kcols], NT, preferred_element_type=f32)
                s_l = jnp.where(mask_l, s_l * scale, LOW)
                s_r = jnp.where(mask_r, s_r * scale, LOW)
                top = jnp.max(jnp.maximum(s_l, s_r), axis=-1, keepdims=True)
                p_l = jnp.exp(s_l - top)
                p_r = jnp.exp(s_r - top)
                total = jnp.sum(p_l + p_r, axis=-1, keepdims=True)
                o = jnp.dot(
                    p_l.astype(bf16), kvl[hf, :tok_dev, vcols], preferred_element_type=f32
                ) + jnp.dot(p_r.astype(bf16), kvr[hf, :, vcols], preferred_element_type=f32)
                o = (o / total).astype(bf16)
                part[hf, q0 : q0 + per_chunk, gl] = o.reshape(per_chunk, block, head_dim)
                lses.append(top + jnp.log(total))
            which = lax.broadcasted_iota(jnp.int32, (chunk_rows, 128), 1)
            packed = jnp.where(which == 0, lses[0], jnp.where(which == 1, lses[1], 0.0))
            stat[hf, q0 // per_chunk] = packed.T[:8, :]
            for i in range(q0, q0 + per_chunk):
                if i > 0:
                    p_copies[hf, i] = (
                        remote(
                            part.at[hf, i],
                            rpart.at[hf, i],
                            ps_sem.at[hf, i],
                            pr_sem.at[hf, i],
                            peer(behind(i)),
                        ),
                        remote(
                            stat.at[hf, i // per_chunk],
                            rstat.at[hf, i],
                            ss_sem.at[hf, i],
                            sr_sem.at[hf, i],
                            peer(behind(i)),
                        ),
                    )

    kc_load.wait()
    vc_load.wait()
    row_of = lax.broadcasted_iota(jnp.int32, (block, 128), 0) % rows_here
    place = lax.broadcasted_iota(jnp.int32, (block, 128), 1)
    visible = [(row_of == r) & (place < cache_length[0:1, r : r + 1]) for r in range(rows_here)]
    own = []
    for g in range(kv_heads):
        hf, gl = g // per_half, g % per_half
        q = qall[0, g]
        s_c = jnp.full((block, 128), LOW, f32)
        for r in range(rows_here):
            s = lax.dot_general(q, kc[r, g], NT, preferred_element_type=f32) * scale
            s_c = jnp.where(visible[r], s, s_c)
        new = kvl[hf, tok_dev : tok_dev + 16, :].astype(f32)[:rows_here]
        k_new = new[:, gl * head_dim : (gl + 1) * head_dim]
        v_new = new[:, half + gl * head_dim : half + (gl + 1) * head_dim]
        k_new = jnp.concatenate([k_new] * (block // rows_here), axis=0)
        v_new = jnp.concatenate([v_new] * (block // rows_here), axis=0)
        s_o = jnp.sum(q.astype(f32) * k_new, axis=-1, keepdims=True) * scale
        top = jnp.maximum(jnp.max(s_c, axis=-1, keepdims=True), s_o)
        p_c = jnp.exp(s_c - top)
        p_o = jnp.exp(s_o - top)
        total = jnp.sum(p_c, axis=-1, keepdims=True) + p_o
        acc = p_o.astype(bf16).astype(f32) * v_new
        for r in range(rows_here):
            acc = acc + jnp.dot(
                jnp.where(row_of == r, p_c, 0.0).astype(bf16), vc[r, g], preferred_element_type=f32
            )
        own.append((top, total, acc))

    for hf in range(2):
        for i in range(1, nk):
            for c in p_copies[hf, i]:
                c.wait_recv()
        rstat[hf, 0] = stat[hf, 0]
        flat = rstat[hf].reshape(nk * 8, 128)
        pad = -(nk * 8) % 128
        if pad:
            flat = jnp.concatenate([flat, jnp.zeros((pad, 128), f32)], axis=0)
        turned = flat.T
        for gl in range(per_half):
            g = hf * per_half + gl
            top, total, acc = own[g]
            cols = []
            for i in range(nk):
                r0 = (i % per_chunk) * block
                cols.append(turned[r0 : r0 + block, i * 8 + gl : i * 8 + gl + 1])
            best = top
            for col in cols:
                best = jnp.maximum(best, col)
            w = jnp.exp(top - best)
            total = total * w
            acc = acc * w
            for i in range(nk):
                w = jnp.exp(cols[i] - best)
                total = total + w
                piece = part[hf, 0, gl] if i == 0 else rpart[hf, i, gl]
                acc = acc + w * piece.astype(f32)
            result = acc / total
            for j in range(group):
                hstage[
                    g * rows_here : (g + 1) * rows_here, j * head_dim : (j + 1) * head_dim
                ] = result[j * rows_here : (j + 1) * rows_here, :]
    hall[me] = hstage[...].astype(bf16)

    h_copies = {}
    for i in range(1, nk):
        h_copies[i] = remote(
            hall.at[me], hall.at[me], hs_sem.at[i], hr_sem.at[i], peer(ahead(i))
        )
    f_copies = {}
    f_copies[0] = remote(hall.at[me], hall.at[me], fs_sem.at[0], fr_sem.at[0], {"seq": sibling})
    for i in range(1, nk):
        h_copies[i].wait_recv()
        at = behind(i) * 2 + mec
        f_copies[i] = remote(
            hall.at[at], hall.at[at], fs_sem.at[i], fr_sem.at[i], {"seq": sibling}
        )
    ow_load.wait()
    for i in range(nk):
        f_copies[i].wait_recv()

    rows_all = hall.shape[0] * 16
    flat = hall[...].reshape(rows_all, hall.shape[2])
    slot_at = lax.broadcasted_iota(jnp.int32, (slot_total, rows_all), 0)
    row_at = lax.broadcasted_iota(jnp.int32, (slot_total, rows_all), 1)
    acc = None
    for g in range(kv_heads):
        want = (slot_at // rows_here) * 16 + g * rows_here + slot_at % rows_here
        pick = jnp.where(row_at == want, 1.0, 0.0).astype(bf16)
        a = jnp.dot(pick, flat, preferred_element_type=f32).astype(bf16)
        span = group * head_dim
        term = lax.dot_general(
            a, ow[:, g * span : (g + 1) * span], NT, preferred_element_type=f32
        )
        acc = term if acc is None else acc + term
    out[...] = acc.astype(bf16)

    for i in range(1, nk):
        q_copies[i].wait_send()
        h_copies[i].wait_send()
        for hf in range(2):
            for c in p_copies[hf, i]:
                c.wait_send()
    for i in range(nk):
        f_copies[i].wait_send()
    slot_copy.wait_send()
    for c in kv_copies:
        c.wait_send()


def body(
    tokens,
    token_request,
    request_slot,
    new_rows,
    queries,
    key_cache,
    value_cache,
    cache_length,
    norm_gain,
    key_weight,
    value_weight,
    key_bias,
    value_bias,
    out_weight,
):
    seq_count = lax.axis_size("seq")
    nk = seq_count // 2
    rows_here, kv_heads, cache_size, head_dim = key_cache.shape
    slot_count = request_slot.shape[0]
    tok_dev, width = tokens.shape
    group = queries.shape[1] // (kv_heads * head_dim)
    kv_width = kv_heads * head_dim
    block = 32
    f32, bf16, i32 = jnp.float32, jnp.bfloat16, jnp.int32
    vmem = pl.BlockSpec(memory_space=pltpu.VMEM)
    hbm = pl.BlockSpec(memory_space=pltpu.HBM)
    dma = pltpu.SemaphoreType.DMA
    dims = (nk, rows_here, kv_heads, group, head_dim)
    return pl.pallas_call(
        functools.partial(kernel, dims),
        out_shape=jax.ShapeDtypeStruct((slot_count, out_weight.shape[1]), bf16),
        in_specs=[hbm] * 14,
        out_specs=vmem,
        scratch_shapes=[
            pltpu.VMEM((1, tok_dev), i32),
            pltpu.VMEM((1, slot_count), i32),
            pltpu.VMEM(new_rows.shape, bf16),
            pltpu.VMEM(queries.shape, bf16),
            pltpu.VMEM((1, rows_here), i32),
            pltpu.VMEM((width // 128, 128), f32),
            pltpu.VMEM((1, kv_width), f32),
            pltpu.VMEM((1, kv_width), f32),
            pltpu.VMEM((1, width), f32),
            pltpu.VMEM((tok_dev, width), bf16),
            pltpu.VMEM((width, kv_width), bf16),
            pltpu.VMEM((width, kv_width), bf16),
            pltpu.VMEM(out_weight.shape[::-1], bf16),
            pltpu.VMEM(key_cache.shape, bf16),
            pltpu.VMEM(value_cache.shape, bf16),
            pltpu.VMEM((tok_dev + 16, width), bf16),
            pltpu.VMEM((kv_heads, block, head_dim), f32),
            pltpu.VMEM((nk, kv_heads, block, head_dim), bf16),
            pltpu.VMEM((2, 8, tok_dev), i32),
            pltpu.VMEM((2, tok_dev + 16, kv_width), bf16),
            pltpu.VMEM((2, tok_dev, kv_width), bf16),
            pltpu.VMEM((2, nk, kv_heads // 2, block, head_dim), bf16),
            pltpu.VMEM((2, nk, kv_heads // 2, block, head_dim), bf16),
            pltpu.VMEM((2, nk // 4, 8, 128), f32),
            pltpu.VMEM((2, nk, 8, 128), f32),
            pltpu.VMEM((16, group * head_dim), f32),
            pltpu.VMEM((seq_count, 16, group * head_dim), bf16),
            dma((17,)),
            dma((nk,)),
            dma((nk,)),
            dma((3,)),
            dma((3,)),
            dma((2, nk)),
            dma((2, nk)),
            dma((2, nk)),
            dma((2, nk)),
            dma((nk,)),
            dma((nk,)),
            dma((nk,)),
            dma((nk,)),
        ],
        compiler_params=pltpu.CompilerParams(
            collective_id=0, has_side_effects=True, vmem_limit_bytes=64 * 1024 * 1024
        ),
    )(
        token_request.reshape(1, tok_dev),
        request_slot.reshape(1, slot_count),
        new_rows,
        queries,
        cache_length.reshape(1, rows_here),
        norm_gain.reshape(width // 128, 128),
        key_bias.reshape(1, kv_width),
        value_bias.reshape(1, kv_width),
        tokens,
        key_weight,
        value_weight,
        out_weight.T,
        key_cache,
        value_cache,
    )


def solution(mesh):
    in_specs = (
        P(("groups", "seq"), None),
        P(("groups", "seq"), None),
        P("groups"),
        P(("groups", "seq"), None),
        P(("groups", "seq"), None),
        P(("groups", "seq"), None, None, None),
        P(("groups", "seq"), None, None, None),
        P(("groups", "seq")),
        P(),
        P(),
        P(),
        P(),
        P(),
        P(None, "seq"),
    )
    out_specs = P("groups", "seq")
    return jax.shard_map(body, mesh=mesh, in_specs=in_specs, out_specs=out_specs, check_vma=False)
```

```python
import functools

import jax
import jax.numpy as jnp
from jax import lax
from jax.experimental import pallas as pl
from jax.experimental.pallas import tpu as pltpu
from jax.sharding import PartitionSpec as P

MESH = pl.DeviceIdType.MESH
NT = (((1,), (1,)), ((), ()))
LOW = -1e30


def kernel(
    dims,
    token_request_hbm,
    request_slot_hbm,
    new_rows_hbm,
    queries_hbm,
    cache_length_hbm,
    norm_gain_hbm,
    key_bias_hbm,
    value_bias_hbm,
    tokens_hbm,
    key_weight_hbm,
    value_weight_hbm,
    out_weight_hbm,
    key_cache_hbm,
    value_cache_hbm,
    out,
    token_request,
    request_slot,
    new_rows,
    queries,
    cache_length,
    norm_gain,
    key_bias,
    value_bias,
    gain_row,
    tok,
    kw,
    vw,
    ow,
    kc,
    vc,
    xn,
    qstage,
    qall,
    slots,
    kvl,
    kvr,
    part,
    rpart,
    hstage,
    hall,
    load_sem,
    qs_sem,
    qr_sem,
    sib_s,
    sib_r,
    ps_sem,
    pr_sem,
    hs_sem,
    hr_sem,
    fs_sem,
    fr_sem,
):
    nk, rows_here, kv_heads, group, head_dim = dims
    f32, bf16 = jnp.float32, jnp.bfloat16
    tok_dev, width = tok.shape
    block = qall.shape[2]
    chunks = 4
    chunk = tok_dev // chunks
    me = lax.axis_index("seq")
    mek, mec = me // 2, me % 2
    sibling = mek * 2 + (1 - mec)

    def ahead(i):
        return lax.rem(mek + i, nk)

    def behind(i):
        return lax.rem(mek + nk - i, nk)

    def peer(k):
        return {"seq": k * 2 + mec}

    loads = []

    def load(src, dst):
        c = pltpu.make_async_copy(src, dst, load_sem.at[len(loads)])
        c.start()
        loads.append(c)
        return c

    q_load = load(queries_hbm, queries)
    request_load = load(token_request_hbm, token_request)
    slot_load = load(request_slot_hbm, request_slot)
    small_loads = [
        load(norm_gain_hbm, norm_gain),
        load(new_rows_hbm, new_rows),
        load(cache_length_hbm, cache_length),
        load(key_bias_hbm, key_bias),
        load(value_bias_hbm, value_bias),
    ]
    tok_loads = [
        load(tokens_hbm.at[pl.ds(c * chunk, chunk)], tok.at[pl.ds(c * chunk, chunk)])
        for c in range(chunks)
    ]
    kw_load = load(key_weight_hbm, kw)
    vw_load = load(value_weight_hbm, vw)
    kc_load = load(key_cache_hbm, kc)
    vc_load = load(value_cache_hbm, vc)
    ow_load = load(out_weight_hbm, ow)

    barrier = pltpu.get_barrier_semaphore()
    pl.semaphore_signal(barrier, inc=1, device_id={"seq": sibling}, device_id_type=MESH)
    for i in range(1, nk):
        pl.semaphore_signal(barrier, inc=1, device_id=peer(ahead(i)), device_id_type=MESH)

    qstage[...] = jnp.zeros_like(qstage)
    q_load.wait()
    q_wide = queries[...].astype(f32)
    for g in range(kv_heads):
        for j in range(group):
            h = g * group + j
            qstage[g, j * rows_here : (j + 1) * rows_here, :] = q_wide[
                :, h * head_dim : (h + 1) * head_dim
            ]
    for g in range(kv_heads):
        qall[0, g] = qstage[g].astype(bf16)

    slot_total = request_slot.shape[1]
    request_load.wait()
    slot_load.wait()
    square = (slot_total, slot_total)
    slot_column = jnp.sum(
        jnp.where(
            lax.broadcasted_iota(jnp.int32, square, 0) == lax.broadcasted_iota(jnp.int32, square, 1),
            request_slot[...].astype(f32),
            0.0,
        ),
        axis=1,
        keepdims=True,
    )
    matches = token_request[...] == lax.broadcasted_iota(jnp.int32, (slot_total, tok_dev), 0)
    slot_row = jnp.sum(
        jnp.where(matches, slot_column, 0.0), axis=0, keepdims=True
    ).astype(jnp.int32)
    slots[0] = jnp.broadcast_to(slot_row, (8, tok_dev))

    pl.semaphore_wait(barrier, nk)

    def remote(src, dst, s, r, device):
        c = pltpu.make_async_remote_copy(
            src_ref=src, dst_ref=dst, send_sem=s, recv_sem=r, device_id=device, device_id_type=MESH
        )
        c.start()
        return c

    started = []
    q_copies = {}
    for i in range(1, nk):
        q_copies[i] = remote(qall.at[0], qall.at[i], qs_sem.at[i], qr_sem.at[i], peer(ahead(i)))
    slot_copy = remote(slots.at[0], slots.at[1], sib_s.at[2], sib_r.at[2], {"seq": sibling})

    for c in small_loads:
        c.wait()
    lanes = norm_gain.shape[1]
    for n in range(norm_gain.shape[0]):
        gain_row[:, n * lanes : (n + 1) * lanes] = norm_gain[n : n + 1, :]
    gain = gain_row[...]

    def normed(x):
        power = jnp.mean(x * x, axis=-1, keepdims=True)
        return (x * lax.rsqrt(power + 1e-06) * gain).astype(bf16)

    fresh = jnp.concatenate(
        [new_rows[...].astype(f32), jnp.zeros((16 - rows_here, width), f32)], axis=0
    )
    xn[tok_dev : tok_dev + 16, :] = normed(fresh)
    for c in range(chunks):
        tok_loads[c].wait()
        if c < chunks // 2:

            @pl.loop(c * chunk // 16, (c + 1) * chunk // 16, unroll=2)
            def _(b):
                at = pl.ds(pl.multiple_of(b * 16, 16), 16)
                xn[at, :] = normed(tok[at, :].astype(f32))

    kw_load.wait()
    vw_load.wait()
    half = kw.shape[1] // 2
    middle = tok_dev // 2

    def project(hf, n, low, high):
        cols = slice(hf * half, (hf + 1) * half)
        w, b = ((kw, key_bias), (vw, value_bias))[n]
        kvl[hf, low:high, n * half : (n + 1) * half] = (
            jnp.dot(xn[low:high, :], w[:, cols], preferred_element_type=f32) + b[:, cols]
        ).astype(bf16)

    left = list(range(middle, tok_dev, 16))
    for n in range(4):
        for at in left[n * len(left) // 4 : (n + 1) * len(left) // 4]:
            xn[at : at + 16, :] = normed(tok[at : at + 16, :].astype(f32))
        project(n // 2, n % 2, 0, middle)
    kv_copies = []
    for hf in range(2):
        for n in range(2):
            project(hf, n, middle, tok_dev + 16)
        kv_copies.append(
            remote(
                kvl.at[hf, pl.ds(0, tok_dev)],
                kvr.at[hf],
                sib_s.at[hf],
                sib_r.at[hf],
                {"seq": sibling},
            )
        )

    for i in range(1, nk):
        q_copies[i].wait_recv()
    slot_copy.wait_recv()

    scale = head_dim ** (-0.5)
    per_half = kv_heads // 2
    per_chunk = min(4, nk)
    chunk_rows = per_chunk * block
    p_copies = {}
    lse_of = [{} for _ in range(nk // per_chunk)]
    for hf in range(2):
        kv_copies[hf].wait_recv()
        for q0 in range(0, nk, per_chunk):
            lane = lax.broadcasted_iota(jnp.int32, (block, 128), 0) % rows_here
            row_slot = jnp.concatenate(
                [(behind(q0 + i) * 2 + mec) * rows_here + lane for i in range(per_chunk)], axis=0
            )[:, :1]
            mask_l = row_slot == slots[0, 0:1, :]
            mask_r = row_slot == slots[1, 0:1, :]
            lses = []
            for gl in range(per_half):
                g = hf * per_half + gl
                q = qall[q0 : q0 + per_chunk, g].reshape(chunk_rows, head_dim)
                kcols = slice(gl * head_dim, (gl + 1) * head_dim)
                vcols = slice(half + gl * head_dim, half + (gl + 1) * head_dim)
                s_l = lax.dot_general(q, kvl[hf, :tok_dev, kcols], NT, preferred_element_type=f32)
                s_r = lax.dot_general(q, kvr[hf, :, kcols], NT, preferred_element_type=f32)
                s_l = jnp.where(mask_l, s_l * scale, LOW)
                s_r = jnp.where(mask_r, s_r * scale, LOW)
                top = jnp.max(jnp.maximum(s_l, s_r), axis=-1, keepdims=True)
                p_l = jnp.exp(s_l - top)
                p_r = jnp.exp(s_r - top)
                total = jnp.sum(p_l + p_r, axis=-1, keepdims=True)
                o = jnp.dot(
                    p_l.astype(bf16), kvl[hf, :tok_dev, vcols], preferred_element_type=f32
                ) + jnp.dot(p_r.astype(bf16), kvr[hf, :, vcols], preferred_element_type=f32)
                o = (o / total).astype(bf16)
                part[q0 : q0 + per_chunk, g] = o.reshape(per_chunk, block, head_dim)
                lses.append(top + jnp.log(total))
            for gl in range(per_half):
                lse_of[q0 // per_chunk][hf * per_half + gl] = lses[gl]
    for c in range(nk // per_chunk):
        which = lax.broadcasted_iota(jnp.int32, (chunk_rows, 128), 1)
        packed = jnp.zeros((chunk_rows, 128), f32)
        for g in range(kv_heads):
            packed = jnp.where(which == g, lse_of[c][g], packed)
        rest = packed.T[:8, :]
        terms = []
        for _ in range(3):
            term = rest.astype(bf16).astype(f32)
            terms.append(term)
            rest = rest - term
        coded = jnp.concatenate(terms + [jnp.zeros((block - 24, 128), f32)], axis=0).astype(bf16)
        for i in range(c * per_chunk, (c + 1) * per_chunk):
            part[i, kv_heads] = coded
            if i > 0:
                p_copies[i] = remote(
                    part.at[i], rpart.at[i], ps_sem.at[i], pr_sem.at[i], peer(behind(i))
                )

    kc_load.wait()
    vc_load.wait()
    row_of = lax.broadcasted_iota(jnp.int32, (block, 128), 0) % rows_here
    place = lax.broadcasted_iota(jnp.int32, (block, 128), 1)
    visible = [(row_of == r) & (place < cache_length[0:1, r : r + 1]) for r in range(rows_here)]
    own = []
    for g in range(kv_heads):
        hf, gl = g // per_half, g % per_half
        q = qall[0, g]
        s_c = jnp.full((block, 128), LOW, f32)
        for r in range(rows_here):
            s = lax.dot_general(q, kc[r, g], NT, preferred_element_type=f32) * scale
            s_c = jnp.where(visible[r], s, s_c)
        new = kvl[hf, tok_dev : tok_dev + 16, :].astype(f32)[:rows_here]
        k_new = new[:, gl * head_dim : (gl + 1) * head_dim]
        v_new = new[:, half + gl * head_dim : half + (gl + 1) * head_dim]
        k_new = jnp.concatenate([k_new] * (block // rows_here), axis=0)
        v_new = jnp.concatenate([v_new] * (block // rows_here), axis=0)
        s_o = jnp.sum(q.astype(f32) * k_new, axis=-1, keepdims=True) * scale
        top = jnp.maximum(jnp.max(s_c, axis=-1, keepdims=True), s_o)
        p_c = jnp.exp(s_c - top)
        p_o = jnp.exp(s_o - top)
        total = jnp.sum(p_c, axis=-1, keepdims=True) + p_o
        acc = p_o.astype(bf16).astype(f32) * v_new
        for r in range(rows_here):
            acc = acc + jnp.dot(
                jnp.where(row_of == r, p_c, 0.0).astype(bf16), vc[r, g], preferred_element_type=f32
            )
        own.append((top, total, acc))

    for i in range(1, nk):
        p_copies[i].wait_recv()
    stats = []
    for i in range(nk):
        coded = (rpart[i, kv_heads] if i > 0 else part[0, kv_heads]).astype(f32)
        stats.append(coded[0:8] + coded[8:16] + coded[16:24])
    flat = jnp.concatenate(stats, axis=0)
    pad = -(nk * 8) % 128
    if pad:
        flat = jnp.concatenate([flat, jnp.zeros((pad, 128), f32)], axis=0)
    turned = flat.T
    for hf in range(2):
        for gl in range(per_half):
            g = hf * per_half + gl
            top, total, acc = own[g]
            cols = []
            for i in range(nk):
                r0 = (i % per_chunk) * block
                cols.append(turned[r0 : r0 + block, i * 8 + g : i * 8 + g + 1])
            best = top
            for col in cols:
                best = jnp.maximum(best, col)
            w = jnp.exp(top - best)
            total = total * w
            acc = acc * w
            for i in range(nk):
                w = jnp.exp(cols[i] - best)
                total = total + w
                piece = part[0, g] if i == 0 else rpart[i, g]
                acc = acc + w * piece.astype(f32)
            result = acc / total
            for j in range(group):
                hstage[
                    g * rows_here : (g + 1) * rows_here, j * head_dim : (j + 1) * head_dim
                ] = result[j * rows_here : (j + 1) * rows_here, :]
    hall[me] = hstage[...].astype(bf16)

    h_copies = {}
    for i in range(1, nk):
        h_copies[i] = remote(
            hall.at[me], hall.at[me], hs_sem.at[i], hr_sem.at[i], peer(ahead(i))
        )
    f_copies = {}
    f_copies[0] = remote(hall.at[me], hall.at[me], fs_sem.at[0], fr_sem.at[0], {"seq": sibling})
    for i in range(1, nk):
        h_copies[i].wait_recv()
        at = behind(i) * 2 + mec
        f_copies[i] = remote(
            hall.at[at], hall.at[at], fs_sem.at[i], fr_sem.at[i], {"seq": sibling}
        )
    ow_load.wait()
    for i in range(nk):
        f_copies[i].wait_recv()

    rows_all = hall.shape[0] * 16
    flat = hall[...].reshape(rows_all, hall.shape[2])
    slot_at = lax.broadcasted_iota(jnp.int32, (slot_total, rows_all), 0)
    row_at = lax.broadcasted_iota(jnp.int32, (slot_total, rows_all), 1)
    acc = None
    for g in range(kv_heads):
        want = (slot_at // rows_here) * 16 + g * rows_here + slot_at % rows_here
        pick = jnp.where(row_at == want, 1.0, 0.0).astype(bf16)
        a = jnp.dot(pick, flat, preferred_element_type=f32).astype(bf16)
        span = group * head_dim
        term = lax.dot_general(
            a, ow[:, g * span : (g + 1) * span], NT, preferred_element_type=f32
        )
        acc = term if acc is None else acc + term
    out[...] = acc.astype(bf16)

    for i in range(1, nk):
        q_copies[i].wait_send()
        h_copies[i].wait_send()
        p_copies[i].wait_send()
    for i in range(nk):
        f_copies[i].wait_send()
    slot_copy.wait_send()
    for c in kv_copies:
        c.wait_send()


def body(
    tokens,
    token_request,
    request_slot,
    new_rows,
    queries,
    key_cache,
    value_cache,
    cache_length,
    norm_gain,
    key_weight,
    value_weight,
    key_bias,
    value_bias,
    out_weight,
):
    seq_count = lax.axis_size("seq")
    nk = seq_count // 2
    rows_here, kv_heads, cache_size, head_dim = key_cache.shape
    slot_count = request_slot.shape[0]
    tok_dev, width = tokens.shape
    group = queries.shape[1] // (kv_heads * head_dim)
    kv_width = kv_heads * head_dim
    block = 32
    f32, bf16, i32 = jnp.float32, jnp.bfloat16, jnp.int32
    vmem = pl.BlockSpec(memory_space=pltpu.VMEM)
    hbm = pl.BlockSpec(memory_space=pltpu.HBM)
    dma = pltpu.SemaphoreType.DMA
    dims = (nk, rows_here, kv_heads, group, head_dim)
    return pl.pallas_call(
        functools.partial(kernel, dims),
        out_shape=jax.ShapeDtypeStruct((slot_count, out_weight.shape[1]), bf16),
        in_specs=[hbm] * 14,
        out_specs=vmem,
        scratch_shapes=[
            pltpu.VMEM((1, tok_dev), i32),
            pltpu.VMEM((1, slot_count), i32),
            pltpu.VMEM(new_rows.shape, bf16),
            pltpu.VMEM(queries.shape, bf16),
            pltpu.VMEM((1, rows_here), i32),
            pltpu.VMEM((width // 128, 128), f32),
            pltpu.VMEM((1, kv_width), f32),
            pltpu.VMEM((1, kv_width), f32),
            pltpu.VMEM((1, width), f32),
            pltpu.VMEM((tok_dev, width), bf16),
            pltpu.VMEM((width, kv_width), bf16),
            pltpu.VMEM((width, kv_width), bf16),
            pltpu.VMEM(out_weight.shape[::-1], bf16),
            pltpu.VMEM(key_cache.shape, bf16),
            pltpu.VMEM(value_cache.shape, bf16),
            pltpu.VMEM((tok_dev + 16, width), bf16),
            pltpu.VMEM((kv_heads, block, head_dim), f32),
            pltpu.VMEM((nk, kv_heads, block, head_dim), bf16),
            pltpu.VMEM((2, 8, tok_dev), i32),
            pltpu.VMEM((2, tok_dev + 16, kv_width), bf16),
            pltpu.VMEM((2, tok_dev, kv_width), bf16),
            pltpu.VMEM((nk, kv_heads + 1, block, head_dim), bf16),
            pltpu.VMEM((nk, kv_heads + 1, block, head_dim), bf16),
            pltpu.VMEM((16, group * head_dim), f32),
            pltpu.VMEM((seq_count, 16, group * head_dim), bf16),
            dma((17,)),
            dma((nk,)),
            dma((nk,)),
            dma((3,)),
            dma((3,)),
            dma((nk,)),
            dma((nk,)),
            dma((nk,)),
            dma((nk,)),
            dma((nk,)),
            dma((nk,)),
        ],
        compiler_params=pltpu.CompilerParams(
            collective_id=0, has_side_effects=True, vmem_limit_bytes=64 * 1024 * 1024
        ),
    )(
        token_request.reshape(1, tok_dev),
        request_slot.reshape(1, slot_count),
        new_rows,
        queries,
        cache_length.reshape(1, rows_here),
        norm_gain.reshape(width // 128, 128),
        key_bias.reshape(1, kv_width),
        value_bias.reshape(1, kv_width),
        tokens,
        key_weight,
        value_weight,
        out_weight.T,
        key_cache,
        value_cache,
    )


def solution(mesh):
    in_specs = (
        P(("groups", "seq"), None),
        P(("groups", "seq"), None),
        P("groups"),
        P(("groups", "seq"), None),
        P(("groups", "seq"), None),
        P(("groups", "seq"), None, None, None),
        P(("groups", "seq"), None, None, None),
        P(("groups", "seq")),
        P(),
        P(),
        P(),
        P(),
        P(),
        P(None, "seq"),
    )
    out_specs = P("groups", "seq")
    return jax.shard_map(body, mesh=mesh, in_specs=in_specs, out_specs=out_specs, check_vma=False)
```
